32 devices in a mesh: grp: 2 (over x), req: 16 (over z, y, core).
Axes of the slice: x: 2, y: 2, z: 4, core: 2. Of those that a mesh axis runs over, the one named last changes fastest.
Arguments:
- xbc: bfloat16 [4096, 9216], P(('grp', 'req')), parts along dimension 0, may hold values from -6 to 6
- dt_raw: float32 [4096, 128], P(('grp', 'req')), parts along dimension 0, may hold values from -6 to 6
- conv_weight: float32 [4, 9216], replicated, may hold values from -3 to 3
- conv_bias: float32 [9216], replicated, may hold values from -3 to 3
- dt_bias: float32 [128], replicated, may hold values from -1 to 1
- a_log: float32 [128], replicated, may hold values from -6 to -2.5
- d_skip: float32 [128], replicated, may hold values from 0.5 to 1.5
- cache_states: bfloat16 [96, 128, 8192], P(('grp', 'req')), parts along dimension 0, may hold values from -24 to 24
- cache_tails: bfloat16 [96, 3, 9216], P(('grp', 'req')), parts along dimension 0, may hold values from -6 to 6
- hit_owner: int32 [32], P('grp'), parts along dimension 0, may hold values from 0 to 15, as said below
- hit_slot: int32 [32], P('grp'), parts along dimension 0, may hold values from 0 to 2, as said below
- hit_spans: int32 [32], P('grp'), parts along dimension 0, may hold values from 0 to 4
- request_of: int32 [32], P(('grp', 'req')), parts along dimension 0, may hold values from 0 to 15, each once
Outputs:
- y_out: bfloat16 [4096, 8192], P(('grp', 'req')), parts along dimension 0
- final_state: bfloat16 [32, 128, 8192], P(('grp', 'req')), parts along dimension 0
The draws below stay inside these ranges and needn't reach their ends.
There are 2 independent parts, one for each index of `grp`. The reference program is written for one: setup_inputs(seed, part) draws one part's arguments, and reference() takes and returns one part's arrays. A program takes and returns all parts, laid end to end along the dimension named above; an argument that names none is the same for every part. Nothing has to cross between parts.
Inputs may be any that keep to these rules, and one draw needn't show every extreme that they name: `hit_owner`: owners are skewed: some devices hold the prefixes of several requests, others of none. `hit_slot`: all requests that name the same owner device name the same slot of it. `request_of`: each request stands on exactly one device.
All inputs are finite; a program needn't handle non-finite values.
Results may differ from the reference program's by a relative error of at most 0.0039.
Values may be sent and summed in bfloat16 or wider, within the bound.
A program may use at most 128 MiB of HBM per device.

```python
import jax
import jax.numpy as jnp
from jax import lax

HEADS = 128
HEAD_DIM = 64
GROUPS = 4
NST = 128
CONV_WIDTH = 4
SPAN = 128
SLOTS = 3
INNER = 8192
CONV_CH = 9216
REQUESTS = 16
ROWS = 2048
SLOTS_ALL = 48


def draw_hits(key):
    base = jax.random.fold_in(key, 17)
    first, second, third, fourth = jax.random.split(base, 4)
    left = jax.random.randint(first, (REQUESTS,), 0, REQUESTS)
    right = jax.random.randint(second, (REQUESTS,), 0, REQUESTS)
    skewed = left * right // REQUESTS
    order = jax.random.permutation(third, REQUESTS)
    owners = order[skewed]
    owners = owners.at[0].set(REQUESTS - 1)
    owners = owners.at[1].set(0)
    served = jax.random.randint(fourth, (REQUESTS,), 0, SLOTS)
    served = served.at[REQUESTS - 1].set(SLOTS - 1)
    served = served.at[0].set(0)
    slots = served[owners]
    return (owners.astype(jnp.int32), slots.astype(jnp.int32))


def draw_hit_owner(key, part):
    return draw_hits(key)[0]


def draw_hit_slot(key, part):
    return draw_hits(key)[1]


def plant(result, rng, smallest, largest):
    longest = result.shape.index(max(result.shape))
    spots = []
    for shift in (0, 1):
        where = [jax.random.randint(jax.random.fold_in(rng, axis), (), 0, length) for axis, length in enumerate(result.shape)]
        where[longest] = (where[longest] + shift) % result.shape[longest]
        spots.append(tuple(where))
    return result.at[spots[0]].set(smallest).at[spots[1]].set(largest)


def level_of(stream_key, shape, cuts, least, high):
    factor_of = 1.0
    for dim, shards_of in cuts:
        steps = jax.random.uniform(jax.random.fold_in(jax.random.fold_in(stream_key, 6), dim), (shards_of,), jnp.float32, least / len(cuts), high / len(cuts))
        factor_of = factor_of * jnp.repeat(jnp.exp(steps), shape[dim] // shards_of).reshape((-1,) + (1,) * (len(shape) - 1 - dim))
    return factor_of


def centred(stream_key, extent, scale, limit, cuts=(), dtype=jnp.bfloat16):
    loudness = level_of(stream_key, extent, cuts, -0.22, 0.18) if cuts else 1.0
    drawn = jax.random.normal(stream_key, extent, jnp.float32) * scale * loudness
    return jnp.minimum(jnp.maximum(drawn, -limit), limit).astype(dtype)


def setup_inputs(seed: int = 0, part: int = 0) -> dict:
    key_of = jax.random.split(jax.random.key(seed), 14)
    part_splits = jax.random.split(jax.random.fold_in(key_of[13], part), 14)
    xbc = centred(part_splits[0], (ROWS, CONV_CH), 1.0, 6.0, ((0, 16),))
    dt_raw = centred(part_splits[1], (ROWS, HEADS), 1.5, 6.0, ((0, 16),), jnp.float32)
    conv_weight = centred(key_of[2], (CONV_WIDTH, CONV_CH), CONV_WIDTH ** -0.5, 3.0, (), jnp.float32)
    conv_bias = centred(key_of[3], (CONV_CH,), 0.5, 3.0, (), jnp.float32)
    dt_bias = jnp.clip(jax.random.uniform(key_of[4], (HEADS,), jnp.float32, -1.0, 1.0), -1.0, 1.0)
    a_log = jnp.clip(jax.random.uniform(key_of[5], (HEADS,), jnp.float32, -6.0, -2.5), -6.0, -2.5)
    d_skip = jnp.clip(jax.random.uniform(key_of[6], (HEADS,), jnp.float32, 0.5, 1.5), 0.5, 1.5)
    cache_states = centred(part_splits[7], (SLOTS_ALL, NST, INNER), 4.0, 24.0, ((0, 16),))
    cache_tails = centred(part_splits[8], (SLOTS_ALL, CONV_WIDTH - 1, CONV_CH), 1.0, 6.0, ((0, 16),))
    hit_owner = draw_hit_owner(jax.random.fold_in(jax.random.fold_in(key_of[13], part), 71), part)
    hit_slot = draw_hit_slot(jax.random.fold_in(jax.random.fold_in(key_of[13], part), 71), part)
    hit_spans = plant(jax.random.randint(part_splits[11], (REQUESTS,), 0, 5), jax.random.fold_in(part_splits[11], 1), 0, 4).astype(jnp.int32)
    request_of = jax.random.permutation(part_splits[12], REQUESTS).astype(jnp.int32)
    return {"xbc": xbc, "dt_raw": dt_raw, "conv_weight": conv_weight, "conv_bias": conv_bias, "dt_bias": dt_bias, "a_log": a_log, "d_skip": d_skip, "cache_states": cache_states, "cache_tails": cache_tails, "hit_owner": hit_owner, "hit_slot": hit_slot, "hit_spans": hit_spans, "request_of": request_of}


def scan_request(xrows, dt_rows, tail, start, conv_weight, conv_bias, dt_bias, a_log, d_skip):
    rows = xrows.shape[0]
    taps = conv_weight.shape[0]
    per_group = HEADS // GROUPS
    extended = jnp.concatenate([tail, xrows], axis=0).astype(jnp.float32)
    conv = jnp.zeros((rows, xrows.shape[1]), jnp.float32) + conv_bias[None, :]
    for k in range(taps):
        conv = conv + conv_weight[k][None, :] * extended[k:k + rows]
    conv_out = jax.nn.silu(conv).astype(jnp.bfloat16)
    inputs = conv_out[:, :INNER].reshape(rows, GROUPS, per_group, HEAD_DIM).astype(jnp.float32)
    b_part = conv_out[:, INNER:INNER + GROUPS * NST].reshape(rows, GROUPS, NST).astype(jnp.float32)
    c_part = conv_out[:, INNER + GROUPS * NST:].reshape(rows, GROUPS, NST).astype(jnp.float32)
    step = jax.nn.softplus(dt_rows + dt_bias[None, :])
    cum = jnp.cumsum(step * (-jnp.exp(a_log))[None, :], axis=0)
    scores = jnp.einsum('tgn,sgn->gts', c_part, b_part)
    diff = cum.T[:, :, None] - cum.T[:, None, :]
    causal = lax.broadcasted_iota(jnp.int32, (rows, rows), 0) >= lax.broadcasted_iota(jnp.int32, (rows, rows), 1)
    decay = jnp.where(causal[None], jnp.exp(jnp.minimum(diff, 0.0)), 0.0)
    mixing = (scores[:, None] * decay.reshape(GROUPS, per_group, rows, rows)
              * step.T.reshape(GROUPS, per_group, 1, rows)).astype(jnp.bfloat16)
    y_intra = jnp.einsum('gjts,sgjp->tgjp', mixing.astype(jnp.float32), inputs)
    start_f = start.reshape(NST, GROUPS, per_group, HEAD_DIM).astype(jnp.float32)
    y_state = jnp.einsum('tgn,ngjp->tgjp', c_part, start_f) * jnp.exp(cum).reshape(rows, GROUPS, per_group, 1)
    skip = d_skip.reshape(1, GROUPS, per_group, 1) * inputs
    y_out = (y_intra + y_state + skip).reshape(rows, INNER).astype(jnp.bfloat16)
    last = cum[rows - 1]
    carried = ((jnp.exp(last[None, :] - cum) * step).reshape(rows, GROUPS, per_group, 1) * inputs).astype(jnp.bfloat16)
    fresh = jnp.einsum('sgn,sgjp->ngjp', b_part, carried.astype(jnp.float32))
    kept = jnp.exp(last).reshape(1, GROUPS, per_group, 1) * start_f
    final = (kept + fresh).reshape(NST, INNER).astype(jnp.bfloat16)
    return y_out, final


def reference(xbc, dt_raw, conv_weight, conv_bias, dt_bias, a_log, d_skip, cache_states, cache_tails, hit_owner, hit_slot, hit_spans, request_of):
    def one_request(item):
        xrows, dt_rows, request = item
        row = (hit_owner[request] * SLOTS + hit_slot[request]).astype(jnp.int32)
        live = hit_spans[request] > 0
        tail_row = lax.dynamic_index_in_dim(cache_tails, row, 0, keepdims=False)
        state_row = lax.dynamic_index_in_dim(cache_states, row, 0, keepdims=False)
        tail = jnp.where(live, tail_row, jnp.zeros_like(tail_row))
        start = jnp.where(live, state_row, jnp.zeros_like(state_row))
        return scan_request(xrows, dt_rows, tail, start, conv_weight, conv_bias, dt_bias, a_log, d_skip)

    outputs, finals = lax.map(one_request, (xbc.reshape(REQUESTS, SPAN, CONV_CH),
                                           dt_raw.reshape(REQUESTS, SPAN, HEADS), request_of))
    return outputs.reshape(ROWS, INNER), finals
```

```python
import jax
import jax.numpy as jnp
from jax import lax
from jax.experimental import pallas as pl
from jax.experimental.pallas import tpu as pltpu
from jax.sharding import PartitionSpec as P

HEADS = 128
HEAD_DIM = 64
GROUPS = 4
NST = 128
INNER = 8192
PER_STEP = 16
COLS = PER_STEP * HEAD_DIM
STEPS = HEADS // PER_STEP
STEPS_PER_GROUP = STEPS // GROUPS


def pick_kernel(index_ref, parts_ref, out_ref, sem):
    count = out_ref.shape[0]
    copies = []
    for i in range(count):
        copy = pltpu.make_async_copy(parts_ref.at[index_ref[i]], out_ref.at[i], sem.at[i])
        copy.start()
        copies.append(copy)
    for copy in copies:
        copy.wait()


def pick(parts, index):
    count = index.shape[0]
    return pl.pallas_call(
        pick_kernel,
        out_shape=jax.ShapeDtypeStruct((count,) + parts.shape[1:], parts.dtype),
        in_specs=[pl.BlockSpec(memory_space=pltpu.SMEM), pl.BlockSpec(memory_space=pl.ANY)],
        out_specs=pl.BlockSpec(memory_space=pl.ANY),
        scratch_shapes=[pltpu.SemaphoreType.DMA((count,))],
        name="pick",
    )(index, parts)


def conv_block(pad, x_ref, tail_ref, w_ref, b_ref, width):
    rows = x_ref.shape[0]
    pad[0:8, 0:width] = tail_ref[...]
    pad[8 : 8 + rows, 0:width] = x_ref[...].astype(jnp.float32)
    v = jnp.broadcast_to(b_ref[...], (rows, width))
    for k in range(4):
        v = v + w_ref[k : k + 1, :] * pad[5 + k : 5 + k + rows, 0:width]
    return (v / (1.0 + jnp.exp(-v))).astype(jnp.bfloat16)


def local_kernel(
    x_ref, xb_ref, xc_ref, tx_ref, tb_ref, tc_ref, wx_ref, wb_ref, wc_ref, bx_ref, bb_ref, bc_ref,
    cum_ref, cumt_ref, stept_ref, coef_ref, skip_ref,
    y_ref, fresh_ref, c_out_ref, pad,
):
    rows = x_ref.shape[0]
    b_part = conv_block(pad, xb_ref, tb_ref, wb_ref, bb_ref, NST)
    c_part = conv_block(pad, xc_ref, tc_ref, wc_ref, bc_ref, NST)
    c_out_ref[...] = c_part
    x = conv_block(pad, x_ref, tx_ref, wx_ref, bx_ref, COLS)
    scores = lax.dot_general(c_part, b_part, (((1,), (1,)), ((), ())), preferred_element_type=jnp.float32)
    causal = lax.broadcasted_iota(jnp.int32, (rows, rows), 0) >= lax.broadcasted_iota(jnp.int32, (rows, rows), 1)
    scores = jnp.where(causal, scores, 0.0)
    low = lax.broadcasted_iota(jnp.int32, (rows, 128), 1) < HEAD_DIM
    cum = cum_ref[0]
    coef = coef_ref[0]
    zero = jnp.zeros((rows, 128), jnp.bfloat16)
    carried = []
    for j in range(0, PER_STEP, 2):
        xp = x[:, j * HEAD_DIM : (j + 2) * HEAD_DIM]
        mixes = []
        for h in (j, j + 1):
            decay = jnp.exp(jnp.minimum(cum[:, h : h + 1] - cumt_ref[0, h : h + 1, :], 0.0))
            mixes.append((scores * decay * stept_ref[0, h : h + 1, :]).astype(jnp.bfloat16))
        mix = jnp.concatenate(mixes, axis=1)
        both = jnp.concatenate([jnp.where(low, xp, zero), jnp.where(low, zero, xp)], axis=0)
        xf = xp.astype(jnp.float32)
        sl = slice(j * HEAD_DIM, (j + 2) * HEAD_DIM)
        y_ref[:, sl] = jnp.dot(mix, both, preferred_element_type=jnp.float32) + skip_ref[:, sl] * xf
        carried.append((jnp.where(low, coef[:, j : j + 1], coef[:, j + 1 : j + 2]) * xf).astype(jnp.bfloat16))
    fresh_ref[...] = lax.dot_general(
        b_part, jnp.concatenate(carried, axis=1), (((0,), (0,)), ((), ())), preferred_element_type=jnp.float32
    )


def state_kernel(live_ref, start_ref, y_ref, fresh_ref, c_ref, ecum_ref, elast_ref, y_out_ref, final_ref):
    rows = y_ref.shape[0]
    start = start_ref[...]
    start = jnp.where(live_ref[0] > 0, start, jnp.zeros_like(start))
    low = lax.broadcasted_iota(jnp.int32, (rows, 128), 1) < HEAD_DIM
    ecum = ecum_ref[0]
    ys = jnp.dot(c_ref[...], start, preferred_element_type=jnp.float32)
    for j in range(0, PER_STEP, 2):
        sl = slice(j * HEAD_DIM, (j + 2) * HEAD_DIM)
        factor = jnp.where(low, ecum[:, j : j + 1], ecum[:, j + 1 : j + 2])
        y_out_ref[:, sl] = (y_ref[:, sl] + factor * ys[:, sl]).astype(jnp.bfloat16)
    final_ref[0] = (elast_ref[...] * start.astype(jnp.float32) + fresh_ref[...]).astype(jnp.bfloat16)


def by_step(a):
    return a.reshape(a.shape[0], STEPS, PER_STEP).transpose(1, 0, 2)


def local(
    xbc, dt_raw, conv_weight, conv_bias, dt_bias, a_log, d_skip, cache_states, cache_tails,
    hit_owner, hit_slot, hit_spans, request_of,
):
    count = hit_owner.shape[0]
    rows = xbc.shape[0]
    mine = request_of[0]
    live = (hit_spans[mine] > 0).astype(jnp.int32)
    device = lax.axis_index("req")
    served = jnp.max(jnp.where(hit_owner == device, hit_slot, 0))
    send = lax.dynamic_slice_in_dim(cache_states, served, 1, 0).reshape(count, NST // count, INNER)
    parts = lax.all_to_all(send, "req", split_axis=0, concat_axis=0, tiled=True)

    own_tail = lax.dynamic_slice_in_dim(cache_tails, served, 1, 0)
    every_tail = lax.all_gather(own_tail, "req", axis=0, tiled=True)
    every_request = lax.all_gather(request_of, "req", axis=0, tiled=True)
    chosen = pick(parts, hit_owner[every_request])
    start = lax.all_to_all(chosen, "req", split_axis=0, concat_axis=0, tiled=True).reshape(NST, INNER)

    tail = lax.dynamic_index_in_dim(every_tail, hit_owner[mine], 0, keepdims=False)
    tail = jnp.where(live > 0, tail, jnp.zeros_like(tail)).astype(jnp.float32)
    tail = jnp.pad(tail, ((5, 0), (0, 0)))
    step = jax.nn.softplus(dt_raw + dt_bias[None, :])
    below = jnp.tril(jnp.ones((rows, rows), jnp.float32))
    cum = jnp.dot(below, step * (-jnp.exp(a_log))[None, :], precision=lax.Precision.HIGHEST)
    last = cum[rows - 1]
    coef = jnp.exp(last[None, :] - cum) * step
    skip = jnp.repeat(d_skip, HEAD_DIM)[None, :]
    elast = jnp.repeat(jnp.exp(last), HEAD_DIM)[None, :]
    cumt = cum.T.reshape(STEPS, PER_STEP, rows)
    stept = step.T.reshape(STEPS, PER_STEP, rows)
    bias = conv_bias[None, :]

    first_b, first_c = INNER // NST, INNER // NST + GROUPS
    per = STEPS_PER_GROUP
    triple = lambda r: [
        pl.BlockSpec((r, COLS), lambda i: (0, i)),
        pl.BlockSpec((r, NST), lambda i: (0, first_b + i // per)),
        pl.BlockSpec((r, NST), lambda i: (0, first_c + i // per)),
    ]
    wide = lambda r: pl.BlockSpec((r, COLS), lambda i: (0, i))
    tall = pl.BlockSpec((1, rows, PER_STEP), lambda i: (i, 0, 0))
    flat = pl.BlockSpec((1, PER_STEP, rows), lambda i: (i, 0, 0))
    group = pl.BlockSpec((rows, NST), lambda i: (0, i // per))
    y_local, fresh, c_part = pl.pallas_call(
        local_kernel,
        grid=(STEPS,),
        out_shape=(
            jax.ShapeDtypeStruct((rows, INNER), jnp.float32),
            jax.ShapeDtypeStruct((NST, INNER), jnp.float32),
            jax.ShapeDtypeStruct((rows, GROUPS * NST), jnp.bfloat16),
        ),
        in_specs=triple(rows) + triple(8) + triple(4) + triple(1) + [tall, flat, flat, tall, wide(1)],
        out_specs=(wide(rows), wide(NST), group),
        scratch_shapes=[pltpu.VMEM((8 + rows, COLS), jnp.float32)],
        compiler_params=pltpu.CompilerParams(vmem_limit_bytes=40 * 2**20),
        cost_estimate=pl.CostEstimate(flops=10**9, bytes_accessed=40 * 10**6, transcendentals=4 * 10**6),
        name="local",
    )(xbc, xbc, xbc, tail, tail, tail, conv_weight, conv_weight, conv_weight, bias, bias, bias,
      by_step(cum), cumt, stept, by_step(coef), skip)

    return pl.pallas_call(
        state_kernel,
        grid=(STEPS,),
        out_shape=(
            jax.ShapeDtypeStruct((rows, INNER), jnp.bfloat16),
            jax.ShapeDtypeStruct((1, NST, INNER), jnp.bfloat16),
        ),
        in_specs=[pl.BlockSpec(memory_space=pltpu.SMEM), wide(NST), wide(rows), wide(NST), group, tall, wide(1)],
        out_specs=(wide(rows), pl.BlockSpec((1, NST, COLS), lambda i: (0, 0, i))),
        compiler_params=pltpu.CompilerParams(vmem_limit_bytes=40 * 2**20),
        name="state",
    )(live[None], start, y_local, fresh, c_part, by_step(jnp.exp(cum)), elast)


def solution(mesh):
    rows = P(("grp", "req"), None)
    slots = P(("grp", "req"), None, None)
    in_specs = (
        rows, rows, P(), P(), P(), P(), P(), slots, slots, P("grp"), P("grp"), P("grp"), P(("grp", "req")),
    )
    return jax.shard_map(local, mesh=mesh, in_specs=in_specs, out_specs=(rows, slots), check_vma=False)
```

```python
import jax
import jax.numpy as jnp
from jax import lax
from jax.experimental import pallas as pl
from jax.experimental.pallas import tpu as pltpu
from jax.sharding import PartitionSpec as P

HEADS = 128
HEAD_DIM = 64
GROUPS = 4
NST = 128
INNER = 8192
PER_STEP = 16
COLS = PER_STEP * HEAD_DIM
STEPS = HEADS // PER_STEP
STEPS_PER_GROUP = STEPS // GROUPS


def pick_kernel(index_ref, parts_ref, out_ref, sem):
    count = out_ref.shape[0]
    copies = []
    for i in range(count):
        copy = pltpu.make_async_copy(parts_ref.at[index_ref[i]], out_ref.at[i], sem.at[i])
        copy.start()
        copies.append(copy)
    for copy in copies:
        copy.wait()


def pick(parts, index):
    count = index.shape[0]
    return pl.pallas_call(
        pick_kernel,
        out_shape=jax.ShapeDtypeStruct((count,) + parts.shape[1:], parts.dtype),
        in_specs=[pl.BlockSpec(memory_space=pltpu.SMEM), pl.BlockSpec(memory_space=pltpu.VMEM)],
        out_specs=pl.BlockSpec(memory_space=pl.ANY),
        scratch_shapes=[pltpu.SemaphoreType.DMA((count,))],
        name="pick",
    )(index, parts)


def conv_block(pad, x_ref, tail_ref, w_ref, b_ref, width):
    rows = x_ref.shape[0]
    pad[0:8, 0:width] = tail_ref[...]
    pad[8 : 8 + rows, 0:width] = x_ref[...].astype(jnp.float32)
    v = jnp.broadcast_to(b_ref[...], (rows, width))
    for k in range(4):
        v = v + w_ref[k : k + 1, :] * pad[5 + k : 5 + k + rows, 0:width]
    return (v / (1.0 + jnp.exp(-v))).astype(jnp.bfloat16)


def local_kernel(
    x_ref, xb_ref, xc_ref, tx_ref, tb_ref, tc_ref, wx_ref, wb_ref, wc_ref, bx_ref, bb_ref, bc_ref,
    cum_ref, cumt_ref, stept_ref, coef_ref, skip_ref,
    y_ref, fresh_ref, c_out_ref, pad,
):
    rows = x_ref.shape[0]
    b_part = conv_block(pad, xb_ref, tb_ref, wb_ref, bb_ref, NST)
    c_part = conv_block(pad, xc_ref, tc_ref, wc_ref, bc_ref, NST)
    c_out_ref[...] = c_part
    x = conv_block(pad, x_ref, tx_ref, wx_ref, bx_ref, COLS)
    scores = lax.dot_general(c_part, b_part, (((1,), (1,)), ((), ())), preferred_element_type=jnp.float32)
    causal = lax.broadcasted_iota(jnp.int32, (rows, rows), 0) >= lax.broadcasted_iota(jnp.int32, (rows, rows), 1)
    scores = jnp.where(causal, scores, 0.0)
    low = lax.broadcasted_iota(jnp.int32, (rows, 128), 1) < HEAD_DIM
    cum = cum_ref[0]
    coef = coef_ref[0]
    zero = jnp.zeros((rows, 128), jnp.bfloat16)
    carried = []
    for j in range(0, PER_STEP, 2):
        xp = x[:, j * HEAD_DIM : (j + 2) * HEAD_DIM]
        mixes = []
        for h in (j, j + 1):
            decay = jnp.exp(jnp.minimum(cum[:, h : h + 1] - cumt_ref[0, h : h + 1, :], 0.0))
            mixes.append((scores * decay * stept_ref[0, h : h + 1, :]).astype(jnp.bfloat16))
        mix = jnp.concatenate(mixes, axis=1)
        both = jnp.concatenate([jnp.where(low, xp, zero), jnp.where(low, zero, xp)], axis=0)
        xf = xp.astype(jnp.float32)
        sl = slice(j * HEAD_DIM, (j + 2) * HEAD_DIM)
        y_ref[:, sl] = jnp.dot(mix, both, preferred_element_type=jnp.float32) + skip_ref[:, sl] * xf
        carried.append((jnp.where(low, coef[:, j : j + 1], coef[:, j + 1 : j + 2]) * xf).astype(jnp.bfloat16))
    fresh_ref[...] = lax.dot_general(
        b_part, jnp.concatenate(carried, axis=1), (((0,), (0,)), ((), ())), preferred_element_type=jnp.float32
    )


def state_kernel(live_ref, start_ref, y_ref, fresh_ref, c_ref, ecum_ref, elast_ref, y_out_ref, final_ref):
    rows = y_ref.shape[0]
    start = start_ref[...]
    start = jnp.where(live_ref[0] > 0, start, jnp.zeros_like(start))
    low = lax.broadcasted_iota(jnp.int32, (rows, 128), 1) < HEAD_DIM
    ecum = ecum_ref[0]
    ys = jnp.dot(c_ref[...], start, preferred_element_type=jnp.float32)
    for j in range(0, PER_STEP, 2):
        sl = slice(j * HEAD_DIM, (j + 2) * HEAD_DIM)
        factor = jnp.where(low, ecum[:, j : j + 1], ecum[:, j + 1 : j + 2])
        y_out_ref[:, sl] = (y_ref[:, sl] + factor * ys[:, sl]).astype(jnp.bfloat16)
    final_ref[0] = (elast_ref[...] * start.astype(jnp.float32) + fresh_ref[...]).astype(jnp.bfloat16)


def by_step(a):
    return a.reshape(a.shape[0], STEPS, PER_STEP).transpose(1, 0, 2)


def local(
    xbc, dt_raw, conv_weight, conv_bias, dt_bias, a_log, d_skip, cache_states, cache_tails,
    hit_owner, hit_slot, hit_spans, request_of,
):
    count = hit_owner.shape[0]
    rows = xbc.shape[0]
    mine = request_of[0]
    live = (hit_spans[mine] > 0).astype(jnp.int32)
    device = lax.axis_index("req")
    served = jnp.max(jnp.where(hit_owner == device, hit_slot, 0))
    send = lax.dynamic_slice_in_dim(cache_states, served, 1, 0).reshape(count, NST // count, INNER)
    own_tail = lax.dynamic_slice_in_dim(cache_tails, served, 1, 0)
    own_request = jnp.full((1, 1, own_tail.shape[2]), mine.astype(own_tail.dtype))
    gathered = lax.all_gather(jnp.concatenate([own_tail, own_request], axis=1), "req", axis=0, tiled=True)
    send, gathered = lax.optimization_barrier((send, gathered))
    every_tail, every_request = gathered[:, :3], gathered[:, 3, 0].astype(jnp.int32)
    parts = lax.all_to_all(send, "req", split_axis=0, concat_axis=0, tiled=True)

    chosen = pick(parts, hit_owner[every_request])
    start = lax.all_to_all(chosen, "req", split_axis=0, concat_axis=0, tiled=True).reshape(NST, INNER)

    tail = lax.dynamic_index_in_dim(every_tail, hit_owner[mine], 0, keepdims=False)
    tail = jnp.where(live > 0, tail, jnp.zeros_like(tail)).astype(jnp.float32)
    tail = jnp.pad(tail, ((5, 0), (0, 0)))
    step = jax.nn.softplus(dt_raw + dt_bias[None, :])
    below = jnp.tril(jnp.ones((rows, rows), jnp.float32))
    cum = jnp.dot(below, step * (-jnp.exp(a_log))[None, :], precision=lax.Precision.HIGHEST)
    last = cum[rows - 1]
    coef = jnp.exp(last[None, :] - cum) * step
    skip = jnp.repeat(d_skip, HEAD_DIM)[None, :]
    elast = jnp.repeat(jnp.exp(last), HEAD_DIM)[None, :]
    cumt = cum.T.reshape(STEPS, PER_STEP, rows)
    stept = step.T.reshape(STEPS, PER_STEP, rows)
    bias = conv_bias[None, :]

    first_b, first_c = INNER // NST, INNER // NST + GROUPS
    per = STEPS_PER_GROUP
    triple = lambda r: [
        pl.BlockSpec((r, COLS), lambda i: (0, i)),
        pl.BlockSpec((r, NST), lambda i: (0, first_b + i // per)),
        pl.BlockSpec((r, NST), lambda i: (0, first_c + i // per)),
    ]
    wide = lambda r: pl.BlockSpec((r, COLS), lambda i: (0, i))
    tall = pl.BlockSpec((1, rows, PER_STEP), lambda i: (i, 0, 0))
    flat = pl.BlockSpec((1, PER_STEP, rows), lambda i: (i, 0, 0))
    group = pl.BlockSpec((rows, NST), lambda i: (0, i // per))
    y_local, fresh, c_part = pl.pallas_call(
        local_kernel,
        grid=(STEPS,),
        out_shape=(
            jax.ShapeDtypeStruct((rows, INNER), jnp.float32),
            jax.ShapeDtypeStruct((NST, INNER), jnp.float32),
            jax.ShapeDtypeStruct((rows, GROUPS * NST), jnp.bfloat16),
        ),
        in_specs=triple(rows) + triple(8) + triple(4) + triple(1) + [tall, flat, flat, tall, wide(1)],
        out_specs=(wide(rows), wide(NST), group),
        scratch_shapes=[pltpu.VMEM((8 + rows, COLS), jnp.float32)],
        compiler_params=pltpu.CompilerParams(vmem_limit_bytes=58 * 2**20),
        cost_estimate=pl.CostEstimate(flops=10**9, bytes_accessed=40 * 10**6, transcendentals=4 * 10**6),
        name="local",
    )(xbc, xbc, xbc, tail, tail, tail, conv_weight, conv_weight, conv_weight, bias, bias, bias,
      by_step(cum), cumt, stept, by_step(coef), skip)

    return pl.pallas_call(
        state_kernel,
        grid=(STEPS,),
        out_shape=(
            jax.ShapeDtypeStruct((rows, INNER), jnp.bfloat16),
            jax.ShapeDtypeStruct((1, NST, INNER), jnp.bfloat16),
        ),
        in_specs=[pl.BlockSpec(memory_space=pltpu.SMEM), wide(NST), wide(rows), wide(NST), group, tall, wide(1)],
        out_specs=(wide(rows), pl.BlockSpec((1, NST, COLS), lambda i: (0, 0, i))),
        compiler_params=pltpu.CompilerParams(vmem_limit_bytes=58 * 2**20),
        name="state",
    )(live[None], start, y_local, fresh, c_part, by_step(jnp.exp(cum)), elast)


def solution(mesh):
    rows = P(("grp", "req"), None)
    slots = P(("grp", "req"), None, None)
    in_specs = (
        rows, rows, P(), P(), P(), P(), P(), slots, slots, P("grp"), P("grp"), P("grp"), P(("grp", "req")),
    )
    return jax.shard_map(local, mesh=mesh, in_specs=in_specs, out_specs=(rows, slots), check_vma=False)
```

```python
import jax
import jax.numpy as jnp
from jax import lax
from jax.experimental import pallas as pl
from jax.experimental.pallas import tpu as pltpu
from jax.sharding import PartitionSpec as P

HEADS = 128
HEAD_DIM = 64
GROUPS = 4
NST = 128
INNER = 8192
PER_STEP = 16
COLS = PER_STEP * HEAD_DIM
STEPS = HEADS // PER_STEP
STEPS_PER_GROUP = STEPS // GROUPS


def pick_kernel(index_ref, parts_ref, out_ref, sem):
    count = out_ref.shape[0]
    copies = []
    for i in range(count):
        copy = pltpu.make_async_copy(parts_ref.at[index_ref[i]], out_ref.at[i], sem.at[i])
        copy.start()
        copies.append(copy)
    for copy in copies:
        copy.wait()


def pick(parts, index):
    count = index.shape[0]
    return pl.pallas_call(
        pick_kernel,
        out_shape=jax.ShapeDtypeStruct((count,) + parts.shape[1:], parts.dtype),
        in_specs=[pl.BlockSpec(memory_space=pltpu.SMEM), pl.BlockSpec(memory_space=pltpu.VMEM)],
        out_specs=pl.BlockSpec(memory_space=pl.ANY),
        scratch_shapes=[pltpu.SemaphoreType.DMA((count,))],
        name="pick",
    )(index, parts)


def conv_block(pad, x_ref, tail_ref, w_ref, b_ref, width):
    rows = x_ref.shape[0]
    pad[0:8, 0:width] = tail_ref[...]
    pad[8 : 8 + rows, 0:width] = x_ref[...].astype(jnp.float32)
    v = jnp.broadcast_to(b_ref[...], (rows, width))
    for k in range(4):
        v = v + w_ref[k : k + 1, :] * pad[5 + k : 5 + k + rows, 0:width]
    return (v / (1.0 + jnp.exp(-v))).astype(jnp.bfloat16)


def local_kernel(
    x_ref, xb_ref, xc_ref, tx_ref, tb_ref, tc_ref, wx_ref, wb_ref, wc_ref, bx_ref, bb_ref, bc_ref,
    cum_ref, cumt_ref, stept_ref, coef_ref, skip_ref,
    y_ref, fresh_ref, c_out_ref, pad,
):
    rows = x_ref.shape[0]
    b_part = conv_block(pad, xb_ref, tb_ref, wb_ref, bb_ref, NST)
    c_part = conv_block(pad, xc_ref, tc_ref, wc_ref, bc_ref, NST)
    c_out_ref[...] = c_part
    x = conv_block(pad, x_ref, tx_ref, wx_ref, bx_ref, COLS)
    scores = lax.dot_general(c_part, b_part, (((1,), (1,)), ((), ())), preferred_element_type=jnp.float32)
    causal = lax.broadcasted_iota(jnp.int32, (rows, rows), 0) >= lax.broadcasted_iota(jnp.int32, (rows, rows), 1)
    scores = jnp.where(causal, scores, 0.0)
    low = lax.broadcasted_iota(jnp.int32, (rows, 128), 1) < HEAD_DIM
    cum = cum_ref[0]
    coef = coef_ref[0]
    zero = jnp.zeros((rows, 128), jnp.bfloat16)
    carried = []
    for j in range(0, PER_STEP, 2):
        xp = x[:, j * HEAD_DIM : (j + 2) * HEAD_DIM]
        mixes = []
        for h in (j, j + 1):
            decay = jnp.exp(jnp.minimum(cum[:, h : h + 1] - cumt_ref[0, h : h + 1, :], 0.0))
            mixes.append((scores * decay * stept_ref[0, h : h + 1, :]).astype(jnp.bfloat16))
        mix = jnp.concatenate(mixes, axis=1)
        both = jnp.concatenate([jnp.where(low, xp, zero), jnp.where(low, zero, xp)], axis=0)
        xf = xp.astype(jnp.float32)
        sl = slice(j * HEAD_DIM, (j + 2) * HEAD_DIM)
        y_ref[:, sl] = jnp.dot(mix, both, preferred_element_type=jnp.float32) + skip_ref[:, sl] * xf
        carried.append((jnp.where(low, coef[:, j : j + 1], coef[:, j + 1 : j + 2]) * xf).astype(jnp.bfloat16))
    fresh_ref[...] = lax.dot_general(
        b_part, jnp.concatenate(carried, axis=1), (((0,), (0,)), ((), ())), preferred_element_type=jnp.float32
    )


def state_kernel(live_ref, start_ref, y_ref, fresh_ref, c_ref, ecum_ref, elast_ref, y_out_ref, final_ref):
    rows = y_ref.shape[0]
    start = start_ref[...]
    start = jnp.where(live_ref[0] > 0, start, jnp.zeros_like(start))
    low = lax.broadcasted_iota(jnp.int32, (rows, 128), 1) < HEAD_DIM
    ecum = ecum_ref[0]
    ys = jnp.dot(c_ref[...], start, preferred_element_type=jnp.float32)
    for j in range(0, PER_STEP, 2):
        sl = slice(j * HEAD_DIM, (j + 2) * HEAD_DIM)
        factor = jnp.where(low, ecum[:, j : j + 1], ecum[:, j + 1 : j + 2])
        y_out_ref[:, sl] = (y_ref[:, sl] + factor * ys[:, sl]).astype(jnp.bfloat16)
    final_ref[0] = (elast_ref[...] * start.astype(jnp.float32) + fresh_ref[...]).astype(jnp.bfloat16)


def by_step(a):
    return a.reshape(a.shape[0], STEPS, PER_STEP).transpose(1, 0, 2)


def local(
    xbc, dt_raw, conv_weight, conv_bias, dt_bias, a_log, d_skip, cache_states, cache_tails,
    hit_owner, hit_slot, hit_spans, request_of,
):
    count = hit_owner.shape[0]
    rows = xbc.shape[0]
    mine = request_of[0]
    live = (hit_spans[mine] > 0).astype(jnp.int32)
    device = lax.axis_index("req")
    served = jnp.max(jnp.where(hit_owner == device, hit_slot, 0))
    send = lax.dynamic_slice_in_dim(cache_states, served, 1, 0).reshape(count, NST // count, INNER)
    own_tail = lax.dynamic_slice_in_dim(cache_tails, served, 1, 0)
    own_request = jnp.full((1, 1, own_tail.shape[2]), mine.astype(own_tail.dtype))
    gathered = lax.all_gather(jnp.concatenate([own_tail, own_request], axis=1), "req", axis=0, tiled=True)
    every_tail, every_request = gathered[:, :3], gathered[:, 3, 0].astype(jnp.int32)
    parts = lax.all_to_all(send, "req", split_axis=0, concat_axis=0, tiled=True)

    chosen = pick(parts, hit_owner[every_request])
    start = lax.all_to_all(chosen, "req", split_axis=0, concat_axis=0, tiled=True).reshape(NST, INNER)

    tail = lax.dynamic_index_in_dim(every_tail, hit_owner[mine], 0, keepdims=False)
    tail = jnp.where(live > 0, tail, jnp.zeros_like(tail)).astype(jnp.float32)
    tail = jnp.pad(tail, ((5, 0), (0, 0)))
    step = jax.nn.softplus(dt_raw + dt_bias[None, :])
    below = jnp.tril(jnp.ones((rows, rows), jnp.float32))
    cum = jnp.dot(below, step * (-jnp.exp(a_log))[None, :], precision=lax.Precision.HIGHEST)
    last = cum[rows - 1]
    coef = jnp.exp(last[None, :] - cum) * step
    skip = jnp.repeat(d_skip, HEAD_DIM)[None, :]
    elast = jnp.repeat(jnp.exp(last), HEAD_DIM)[None, :]
    cumt = cum.T.reshape(STEPS, PER_STEP, rows)
    stept = step.T.reshape(STEPS, PER_STEP, rows)
    bias = conv_bias[None, :]

    first_b, first_c = INNER // NST, INNER // NST + GROUPS
    per = STEPS_PER_GROUP
    triple = lambda r: [
        pl.BlockSpec((r, COLS), lambda i: (0, i)),
        pl.BlockSpec((r, NST), lambda i: (0, first_b + i // per)),
        pl.BlockSpec((r, NST), lambda i: (0, first_c + i // per)),
    ]
    wide = lambda r: pl.BlockSpec((r, COLS), lambda i: (0, i))
    tall = pl.BlockSpec((1, rows, PER_STEP), lambda i: (i, 0, 0))
    flat = pl.BlockSpec((1, PER_STEP, rows), lambda i: (i, 0, 0))
    group = pl.BlockSpec((rows, NST), lambda i: (0, i // per))
    y_local, fresh, c_part = pl.pallas_call(
        local_kernel,
        grid=(STEPS,),
        out_shape=(
            jax.ShapeDtypeStruct((rows, INNER), jnp.float32),
            jax.ShapeDtypeStruct((NST, INNER), jnp.float32),
            jax.ShapeDtypeStruct((rows, GROUPS * NST), jnp.bfloat16),
        ),
        in_specs=triple(rows) + triple(8) + triple(4) + triple(1) + [tall, flat, flat, tall, wide(1)],
        out_specs=(wide(rows), wide(NST), group),
        scratch_shapes=[pltpu.VMEM((8 + rows, COLS), jnp.float32)],
        compiler_params=pltpu.CompilerParams(vmem_limit_bytes=58 * 2**20),
        cost_estimate=pl.CostEstimate(flops=10**9, bytes_accessed=40 * 10**6, transcendentals=4 * 10**6),
        name="local",
    )(xbc, xbc, xbc, tail, tail, tail, conv_weight, conv_weight, conv_weight, bias, bias, bias,
      by_step(cum), cumt, stept, by_step(coef), skip)

    return pl.pallas_call(
        state_kernel,
        grid=(STEPS,),
        out_shape=(
            jax.ShapeDtypeStruct((rows, INNER), jnp.bfloat16),
            jax.ShapeDtypeStruct((1, NST, INNER), jnp.bfloat16),
        ),
        in_specs=[pl.BlockSpec(memory_space=pltpu.SMEM), wide(NST), wide(rows), wide(NST), group, tall, wide(1)],
        out_specs=(wide(rows), pl.BlockSpec((1, NST, COLS), lambda i: (0, 0, i))),
        compiler_params=pltpu.CompilerParams(vmem_limit_bytes=58 * 2**20),
        name="state",
    )(live[None], start, y_local, fresh, c_part, by_step(jnp.exp(cum)), elast)


def solution(mesh):
    rows = P(("grp", "req"), None)
    slots = P(("grp", "req"), None, None)
    in_specs = (
        rows, rows, P(), P(), P(), P(), P(), slots, slots, P("grp"), P("grp"), P("grp"), P(("grp", "req")),
    )
    return jax.shard_map(local, mesh=mesh, in_specs=in_specs, out_specs=(rows, slots), check_vma=False)
```

```python
import jax
import jax.numpy as jnp
from jax import lax
from jax.experimental import pallas as pl
from jax.experimental.pallas import tpu as pltpu
from jax.sharding import PartitionSpec as P

HEADS = 128
HEAD_DIM = 64
GROUPS = 4
NST = 128
INNER = 8192
PER_STEP = 16
COLS = PER_STEP * HEAD_DIM
STEPS = HEADS // PER_STEP
STEPS_PER_GROUP = STEPS // GROUPS


def pick_kernel(index_ref, parts_ref, out_ref, sem):
    count = out_ref.shape[0]
    copies = []
    for i in range(count):
        copy = pltpu.make_async_copy(parts_ref.at[index_ref[i], :, pl.ds(0, INNER)], out_ref.at[i], sem.at[i])
        copy.start()
        copies.append(copy)
    for copy in copies:
        copy.wait()


def pick(parts, index):
    count = index.shape[0]
    return pl.pallas_call(
        pick_kernel,
        out_shape=jax.ShapeDtypeStruct((count, parts.shape[1], INNER), parts.dtype),
        in_specs=[pl.BlockSpec(memory_space=pltpu.SMEM), pl.BlockSpec(memory_space=pltpu.VMEM)],
        out_specs=pl.BlockSpec(memory_space=pl.ANY),
        scratch_shapes=[pltpu.SemaphoreType.DMA((count,))],
        compiler_params=pltpu.CompilerParams(vmem_limit_bytes=8 * 2**20),
        name="pick",
    )(index, parts)


def conv_block(pad, x_ref, tail_ref, w_ref, b_ref, width):
    rows = x_ref.shape[0]
    pad[0:8, 0:width] = tail_ref[...]
    pad[8 : 8 + rows, 0:width] = x_ref[...].astype(jnp.float32)
    v = jnp.broadcast_to(b_ref[...], (rows, width))
    for k in range(4):
        v = v + w_ref[k : k + 1, :] * pad[5 + k : 5 + k + rows, 0:width]
    return (v / (1.0 + jnp.exp(-v))).astype(jnp.bfloat16)


def local_kernel(
    x_ref, xb_ref, xc_ref, tx_ref, tb_ref, tc_ref, wx_ref, wb_ref, wc_ref, bx_ref, bb_ref, bc_ref,
    cum_ref, cumt_ref, stept_ref, coef_ref, skip_ref,
    y_ref, fresh_ref, c_out_ref, pad,
):
    rows = x_ref.shape[0]
    b_part = conv_block(pad, xb_ref, tb_ref, wb_ref, bb_ref, NST)
    c_part = conv_block(pad, xc_ref, tc_ref, wc_ref, bc_ref, NST)
    c_out_ref[...] = c_part
    x = conv_block(pad, x_ref, tx_ref, wx_ref, bx_ref, COLS)
    scores = lax.dot_general(c_part, b_part, (((1,), (1,)), ((), ())), preferred_element_type=jnp.float32)
    causal = lax.broadcasted_iota(jnp.int32, (rows, rows), 0) >= lax.broadcasted_iota(jnp.int32, (rows, rows), 1)
    scores = jnp.where(causal, scores, 0.0)
    low = lax.broadcasted_iota(jnp.int32, (rows, 128), 1) < HEAD_DIM
    cum = cum_ref[0]
    coef = coef_ref[0]
    zero = jnp.zeros((rows, 128), jnp.bfloat16)
    carried = []
    for j in range(0, PER_STEP, 2):
        xp = x[:, j * HEAD_DIM : (j + 2) * HEAD_DIM]
        mixes = []
        for h in (j, j + 1):
            decay = jnp.exp(jnp.minimum(cum[:, h : h + 1] - cumt_ref[0, h : h + 1, :], 0.0))
            mixes.append((scores * decay * stept_ref[0, h : h + 1, :]).astype(jnp.bfloat16))
        mix = jnp.concatenate(mixes, axis=1)
        both = jnp.concatenate([jnp.where(low, xp, zero), jnp.where(low, zero, xp)], axis=0)
        xf = xp.astype(jnp.float32)
        sl = slice(j * HEAD_DIM, (j + 2) * HEAD_DIM)
        y_ref[:, sl] = jnp.dot(mix, both, preferred_element_type=jnp.float32) + skip_ref[:, sl] * xf
        carried.append((jnp.where(low, coef[:, j : j + 1], coef[:, j + 1 : j + 2]) * xf).astype(jnp.bfloat16))
    fresh_ref[...] = lax.dot_general(
        b_part, jnp.concatenate(carried, axis=1), (((0,), (0,)), ((), ())), preferred_element_type=jnp.float32
    )


def state_kernel(live_ref, start_ref, y_ref, fresh_ref, c_ref, ecum_ref, elast_ref, y_out_ref, final_ref):
    rows = y_ref.shape[0]
    start = start_ref[...]
    start = jnp.where(live_ref[0] > 0, start, jnp.zeros_like(start))
    low = lax.broadcasted_iota(jnp.int32, (rows, 128), 1) < HEAD_DIM
    ecum = ecum_ref[0]
    ys = jnp.dot(c_ref[...], start, preferred_element_type=jnp.float32)
    for j in range(0, PER_STEP, 2):
        sl = slice(j * HEAD_DIM, (j + 2) * HEAD_DIM)
        factor = jnp.where(low, ecum[:, j : j + 1], ecum[:, j + 1 : j + 2])
        y_out_ref[:, sl] = (y_ref[:, sl] + factor * ys[:, sl]).astype(jnp.bfloat16)
    final_ref[0] = (elast_ref[...] * start.astype(jnp.float32) + fresh_ref[...]).astype(jnp.bfloat16)


def by_step(a):
    return a.reshape(a.shape[0], STEPS, PER_STEP).transpose(1, 0, 2)


def local(
    xbc, dt_raw, conv_weight, conv_bias, dt_bias, a_log, d_skip, cache_states, cache_tails,
    hit_owner, hit_slot, hit_spans, request_of,
):
    count = hit_owner.shape[0]
    rows = xbc.shape[0]
    mine = request_of[0]
    live = (hit_spans[mine] > 0).astype(jnp.int32)
    device = lax.axis_index("req")
    served = jnp.max(jnp.where(hit_owner == device, hit_slot, 0))
    send = lax.dynamic_slice_in_dim(cache_states, served, 1, 0).reshape(count, NST // count, INNER)
    number = jnp.broadcast_to(mine.astype(send.dtype), send.shape[:2] + (128,))
    parts = lax.all_to_all(
        jnp.concatenate([send, number], axis=2), "req", split_axis=0, concat_axis=0, tiled=True
    )
    every_request = parts[:, 0, INNER].astype(jnp.int32)
    own_tail = lax.dynamic_slice_in_dim(cache_tails, served, 1, 0)
    own_tail = jnp.pad(own_tail, ((0, 0), (0, 1), (0, 0)))
    every_tail = lax.all_gather(own_tail, "req", axis=0, tiled=True)[:, :3]
    owners = jnp.sum(
        jnp.where(every_request[:, None] == jnp.arange(count)[None, :], hit_owner[None, :], 0), axis=1
    )
    chosen = pick(parts, owners)
    start = lax.all_to_all(chosen, "req", split_axis=0, concat_axis=0, tiled=True).reshape(NST, INNER)

    tail = lax.dynamic_index_in_dim(every_tail, hit_owner[mine], 0, keepdims=False)
    tail = jnp.where(live > 0, tail, jnp.zeros_like(tail)).astype(jnp.float32)
    tail = jnp.pad(tail, ((5, 0), (0, 0)))
    step = jax.nn.softplus(dt_raw + dt_bias[None, :])
    below = jnp.tril(jnp.ones((rows, rows), jnp.float32))
    cum = jnp.dot(below, step * (-jnp.exp(a_log))[None, :], precision=lax.Precision.HIGHEST)
    last = cum[rows - 1]
    coef = jnp.exp(last[None, :] - cum) * step
    skip = jnp.repeat(d_skip, HEAD_DIM)[None, :]
    elast = jnp.repeat(jnp.exp(last), HEAD_DIM)[None, :]
    cumt = cum.T.reshape(STEPS, PER_STEP, rows)
    stept = step.T.reshape(STEPS, PER_STEP, rows)
    bias = conv_bias[None, :]

    first_b, first_c = INNER // NST, INNER // NST + GROUPS
    per = STEPS_PER_GROUP
    triple = lambda r: [
        pl.BlockSpec((r, COLS), lambda i: (0, i)),
        pl.BlockSpec((r, NST), lambda i: (0, first_b + i // per)),
        pl.BlockSpec((r, NST), lambda i: (0, first_c + i // per)),
    ]
    wide = lambda r: pl.BlockSpec((r, COLS), lambda i: (0, i))
    tall = pl.BlockSpec((1, rows, PER_STEP), lambda i: (i, 0, 0))
    flat = pl.BlockSpec((1, PER_STEP, rows), lambda i: (i, 0, 0))
    group = pl.BlockSpec((rows, NST), lambda i: (0, i // per))
    y_local, fresh, c_part = pl.pallas_call(
        local_kernel,
        grid=(STEPS,),
        out_shape=(
            jax.ShapeDtypeStruct((rows, INNER), jnp.float32),
            jax.ShapeDtypeStruct((NST, INNER), jnp.float32),
            jax.ShapeDtypeStruct((rows, GROUPS * NST), jnp.bfloat16),
        ),
        in_specs=triple(rows) + triple(8) + triple(4) + triple(1) + [tall, flat, flat, tall, wide(1)],
        out_specs=(wide(rows), wide(NST), group),
        scratch_shapes=[pltpu.VMEM((8 + rows, COLS), jnp.float32)],
        compiler_params=pltpu.CompilerParams(vmem_limit_bytes=58 * 2**20),
        cost_estimate=pl.CostEstimate(flops=10**9, bytes_accessed=40 * 10**6, transcendentals=4 * 10**6),
        name="local",
    )(xbc, xbc, xbc, tail, tail, tail, conv_weight, conv_weight, conv_weight, bias, bias, bias,
      by_step(cum), cumt, stept, by_step(coef), skip)

    return pl.pallas_call(
        state_kernel,
        grid=(STEPS,),
        out_shape=(
            jax.ShapeDtypeStruct((rows, INNER), jnp.bfloat16),
            jax.ShapeDtypeStruct((1, NST, INNER), jnp.bfloat16),
        ),
        in_specs=[pl.BlockSpec(memory_space=pltpu.SMEM), wide(NST), wide(rows), wide(NST), group, tall, wide(1)],
        out_specs=(wide(rows), pl.BlockSpec((1, NST, COLS), lambda i: (0, 0, i))),
        compiler_params=pltpu.CompilerParams(vmem_limit_bytes=58 * 2**20),
        name="state",
    )(live[None], start, y_local, fresh, c_part, by_step(jnp.exp(cum)), elast)


def solution(mesh):
    rows = P(("grp", "req"), None)
    slots = P(("grp", "req"), None, None)
    in_specs = (
        rows, rows, P(), P(), P(), P(), P(), slots, slots, P("grp"), P("grp"), P("grp"), P(("grp", "req")),
    )
    return jax.shard_map(local, mesh=mesh, in_specs=in_specs, out_specs=(rows, slots), check_vma=False)
```

```python
import jax
import jax.numpy as jnp
from jax import lax
from jax.experimental import pallas as pl
from jax.experimental.pallas import tpu as pltpu
from jax.sharding import PartitionSpec as P

HEADS = 128
HEAD_DIM = 64
GROUPS = 4
NST = 128
INNER = 8192
PER_STEP = 16
COLS = PER_STEP * HEAD_DIM
STEPS = HEADS // PER_STEP
STEPS_PER_GROUP = STEPS // GROUPS


def pick_kernel(index_ref, parts_ref, out_ref, sem):
    count = out_ref.shape[0]
    copies = []
    for i in range(count):
        copy = pltpu.make_async_copy(parts_ref.at[index_ref[i], :, pl.ds(0, INNER)], out_ref.at[i], sem.at[i])
        copy.start()
        copies.append(copy)
    for copy in copies:
        copy.wait()


def pick(parts, index):
    count = index.shape[0]
    return pl.pallas_call(
        pick_kernel,
        out_shape=jax.ShapeDtypeStruct((count, parts.shape[1], INNER), parts.dtype),
        in_specs=[pl.BlockSpec(memory_space=pltpu.SMEM), pl.BlockSpec(memory_space=pltpu.VMEM)],
        out_specs=pl.BlockSpec(memory_space=pl.ANY),
        scratch_shapes=[pltpu.SemaphoreType.DMA((count,))],
        compiler_params=pltpu.CompilerParams(vmem_limit_bytes=8 * 2**20),
        name="pick",
    )(index, parts)


def conv_block(pad, x_ref, tail_ref, w_ref, b_ref, width):
    rows = x_ref.shape[0]
    pad[0:8, 0:width] = tail_ref[...]
    pad[8 : 8 + rows, 0:width] = x_ref[...].astype(jnp.float32)
    v = jnp.broadcast_to(b_ref[...], (rows, width))
    for k in range(4):
        v = v + w_ref[k : k + 1, :] * pad[5 + k : 5 + k + rows, 0:width]
    return (v / (1.0 + jnp.exp(-v))).astype(jnp.bfloat16)


def local_kernel(
    x_ref, xb_ref, xc_ref, tx_ref, tb_ref, tc_ref, wx_ref, wb_ref, wc_ref, bx_ref, bb_ref, bc_ref,
    cum_ref, cumt_ref, stept_ref, coef_ref, skip_ref,
    y_ref, fresh_ref, c_out_ref, pad,
):
    rows = x_ref.shape[0]
    b_part = conv_block(pad, xb_ref, tb_ref, wb_ref, bb_ref, NST)
    c_part = conv_block(pad, xc_ref, tc_ref, wc_ref, bc_ref, NST)
    c_out_ref[...] = c_part
    x = conv_block(pad, x_ref, tx_ref, wx_ref, bx_ref, COLS)
    scores = lax.dot_general(c_part, b_part, (((1,), (1,)), ((), ())), preferred_element_type=jnp.float32)
    causal = lax.broadcasted_iota(jnp.int32, (rows, rows), 0) >= lax.broadcasted_iota(jnp.int32, (rows, rows), 1)
    scores = jnp.where(causal, scores, 0.0)
    low = lax.broadcasted_iota(jnp.int32, (rows, 128), 1) < HEAD_DIM
    cum = cum_ref[0]
    coef = coef_ref[0]
    zero = jnp.zeros((rows, 128), jnp.bfloat16)
    carried = []
    for j in range(0, PER_STEP, 2):
        xp = x[:, j * HEAD_DIM : (j + 2) * HEAD_DIM]
        mixes = []
        for h in (j, j + 1):
            decay = jnp.exp(jnp.minimum(cum[:, h : h + 1] - cumt_ref[0, h : h + 1, :], 0.0))
            mixes.append((scores * decay * stept_ref[0, h : h + 1, :]).astype(jnp.bfloat16))
        mix = jnp.concatenate(mixes, axis=1)
        both = jnp.concatenate([jnp.where(low, xp, zero), jnp.where(low, zero, xp)], axis=0)
        xf = xp.astype(jnp.float32)
        sl = slice(j * HEAD_DIM, (j + 2) * HEAD_DIM)
        y_ref[:, sl] = jnp.dot(mix, both, preferred_element_type=jnp.float32) + skip_ref[:, sl] * xf
        carried.append((jnp.where(low, coef[:, j : j + 1], coef[:, j + 1 : j + 2]) * xf).astype(jnp.bfloat16))
    fresh_ref[...] = lax.dot_general(
        b_part, jnp.concatenate(carried, axis=1), (((0,), (0,)), ((), ())), preferred_element_type=jnp.float32
    )


def state_kernel(live_ref, start_ref, y_ref, fresh_ref, c_ref, ecum_ref, elast_ref, y_out_ref, final_ref):
    rows = y_ref.shape[0]
    start = start_ref[...]
    start = jnp.where(live_ref[0] > 0, start, jnp.zeros_like(start))
    low = lax.broadcasted_iota(jnp.int32, (rows, 128), 1) < HEAD_DIM
    ecum = ecum_ref[0]
    ys = jnp.dot(c_ref[...], start, preferred_element_type=jnp.float32)
    for j in range(0, PER_STEP, 2):
        sl = slice(j * HEAD_DIM, (j + 2) * HEAD_DIM)
        factor = jnp.where(low, ecum[:, j : j + 1], ecum[:, j + 1 : j + 2])
        y_out_ref[:, sl] = (y_ref[:, sl] + factor * ys[:, sl]).astype(jnp.bfloat16)
    final_ref[0] = (elast_ref[...] * start.astype(jnp.float32) + fresh_ref[...]).astype(jnp.bfloat16)


def by_step(a):
    return a.reshape(a.shape[0], STEPS, PER_STEP).transpose(1, 0, 2)


def local(
    xbc, dt_raw, conv_weight, conv_bias, dt_bias, a_log, d_skip, cache_states, cache_tails,
    hit_owner, hit_slot, hit_spans, request_of,
):
    count = hit_owner.shape[0]
    rows = xbc.shape[0]
    mine = request_of[0]
    live = (hit_spans[mine] > 0).astype(jnp.int32)
    device = lax.axis_index("req")
    served = jnp.max(jnp.where(hit_owner == device, hit_slot, 0))
    own_tail = lax.dynamic_slice_in_dim(cache_tails, served, 1, 0)
    every_tail = lax.all_gather(own_tail, "req", axis=0, tiled=True)
    send = lax.dynamic_slice_in_dim(cache_states, served, 1, 0).reshape(count, NST // count, INNER)
    number = jnp.broadcast_to(mine.astype(send.dtype), send.shape[:2] + (128,))
    send, every_tail = lax.optimization_barrier((jnp.concatenate([send, number], axis=2), every_tail))
    parts = lax.all_to_all(
        send, "req", split_axis=0, concat_axis=0, tiled=True
    )
    every_request = parts[:, 0, INNER].astype(jnp.int32)
    owners = jnp.sum(
        jnp.where(every_request[:, None] == jnp.arange(count)[None, :], hit_owner[None, :], 0), axis=1
    )
    chosen = pick(parts, owners)
    start = lax.all_to_all(chosen, "req", split_axis=0, concat_axis=0, tiled=True).reshape(NST, INNER)

    tail = lax.dynamic_index_in_dim(every_tail, hit_owner[mine], 0, keepdims=False)
    tail = jnp.where(live > 0, tail, jnp.zeros_like(tail)).astype(jnp.float32)
    tail = jnp.pad(tail, ((5, 0), (0, 0)))
    step = jax.nn.softplus(dt_raw + dt_bias[None, :])
    below = jnp.tril(jnp.ones((rows, rows), jnp.float32))
    cum = jnp.dot(below, step * (-jnp.exp(a_log))[None, :], precision=lax.Precision.HIGHEST)
    last = cum[rows - 1]
    coef = jnp.exp(last[None, :] - cum) * step
    skip = jnp.repeat(d_skip, HEAD_DIM)[None, :]
    elast = jnp.repeat(jnp.exp(last), HEAD_DIM)[None, :]
    cumt = cum.T.reshape(STEPS, PER_STEP, rows)
    stept = step.T.reshape(STEPS, PER_STEP, rows)
    bias = conv_bias[None, :]

    first_b, first_c = INNER // NST, INNER // NST + GROUPS
    per = STEPS_PER_GROUP
    triple = lambda r: [
        pl.BlockSpec((r, COLS), lambda i: (0, i)),
        pl.BlockSpec((r, NST), lambda i: (0, first_b + i // per)),
        pl.BlockSpec((r, NST), lambda i: (0, first_c + i // per)),
    ]
    wide = lambda r: pl.BlockSpec((r, COLS), lambda i: (0, i))
    tall = pl.BlockSpec((1, rows, PER_STEP), lambda i: (i, 0, 0))
    flat = pl.BlockSpec((1, PER_STEP, rows), lambda i: (i, 0, 0))
    group = pl.BlockSpec((rows, NST), lambda i: (0, i // per))
    y_local, fresh, c_part = pl.pallas_call(
        local_kernel,
        grid=(STEPS,),
        out_shape=(
            jax.ShapeDtypeStruct((rows, INNER), jnp.float32),
            jax.ShapeDtypeStruct((NST, INNER), jnp.float32),
            jax.ShapeDtypeStruct((rows, GROUPS * NST), jnp.bfloat16),
        ),
        in_specs=triple(rows) + triple(8) + triple(4) + triple(1) + [tall, flat, flat, tall, wide(1)],
        out_specs=(wide(rows), wide(NST), group),
        scratch_shapes=[pltpu.VMEM((8 + rows, COLS), jnp.float32)],
        compiler_params=pltpu.CompilerParams(vmem_limit_bytes=58 * 2**20),
        cost_estimate=pl.CostEstimate(flops=10**9, bytes_accessed=40 * 10**6, transcendentals=4 * 10**6),
        name="local",
    )(xbc, xbc, xbc, tail, tail, tail, conv_weight, conv_weight, conv_weight, bias, bias, bias,
      by_step(cum), cumt, stept, by_step(coef), skip)

    return pl.pallas_call(
        state_kernel,
        grid=(STEPS,),
        out_shape=(
            jax.ShapeDtypeStruct((rows, INNER), jnp.bfloat16),
            jax.ShapeDtypeStruct((1, NST, INNER), jnp.bfloat16),
        ),
        in_specs=[pl.BlockSpec(memory_space=pltpu.SMEM), wide(NST), wide(rows), wide(NST), group, tall, wide(1)],
        out_specs=(wide(rows), pl.BlockSpec((1, NST, COLS), lambda i: (0, 0, i))),
        compiler_params=pltpu.CompilerParams(vmem_limit_bytes=58 * 2**20),
        name="state",
    )(live[None], start, y_local, fresh, c_part, by_step(jnp.exp(cum)), elast)


def solution(mesh):
    rows = P(("grp", "req"), None)
    slots = P(("grp", "req"), None, None)
    in_specs = (
        rows, rows, P(), P(), P(), P(), P(), slots, slots, P("grp"), P("grp"), P("grp"), P(("grp", "req")),
    )
    return jax.shard_map(local, mesh=mesh, in_specs=in_specs, out_specs=(rows, slots), check_vma=False)
```

```python
import jax
import jax.numpy as jnp
from jax import lax
from jax.experimental import pallas as pl
from jax.experimental.pallas import tpu as pltpu
from jax.sharding import PartitionSpec as P

HEADS = 128
HEAD_DIM = 64
GROUPS = 4
NST = 128
INNER = 8192
PER_STEP = 16
COLS = PER_STEP * HEAD_DIM
STEPS = HEADS // PER_STEP
STEPS_PER_GROUP = STEPS // GROUPS


def pick_kernel(index_ref, parts_ref, out_ref, sem):
    count = out_ref.shape[0]
    copies = []
    for i in range(count):
        copy = pltpu.make_async_copy(parts_ref.at[index_ref[i], :, pl.ds(0, INNER)], out_ref.at[i], sem.at[i])
        copy.start()
        copies.append(copy)
    for copy in copies:
        copy.wait()


def pick(parts, index):
    count = index.shape[0]
    return pl.pallas_call(
        pick_kernel,
        out_shape=jax.ShapeDtypeStruct((count, parts.shape[1], INNER), parts.dtype),
        in_specs=[pl.BlockSpec(memory_space=pltpu.SMEM), pl.BlockSpec(memory_space=pltpu.VMEM)],
        out_specs=pl.BlockSpec(memory_space=pl.ANY),
        scratch_shapes=[pltpu.SemaphoreType.DMA((count,))],
        compiler_params=pltpu.CompilerParams(vmem_limit_bytes=8 * 2**20),
        name="pick",
    )(index, parts)


def conv_block(pad, x_ref, tail_ref, w_ref, b_ref, width):
    rows = x_ref.shape[0]
    pad[0:8, 0:width] = tail_ref[...]
    pad[8 : 8 + rows, 0:width] = x_ref[...].astype(jnp.float32)
    v = jnp.broadcast_to(b_ref[...], (rows, width))
    for k in range(4):
        v = v + w_ref[k : k + 1, :] * pad[5 + k : 5 + k + rows, 0:width]
    return (v / (1.0 + jnp.exp(-v))).astype(jnp.bfloat16)


def local_kernel(
    x_ref, xb_ref, xc_ref, tx_ref, tb_ref, tc_ref, wx_ref, wb_ref, wc_ref, bx_ref, bb_ref, bc_ref,
    cum_ref, cumt_ref, stept_ref, coef_ref, skip_ref,
    y_ref, fresh_ref, c_out_ref, pad,
):
    rows = x_ref.shape[0]
    b_part = conv_block(pad, xb_ref, tb_ref, wb_ref, bb_ref, NST)
    c_part = conv_block(pad, xc_ref, tc_ref, wc_ref, bc_ref, NST)
    c_out_ref[...] = c_part
    x = conv_block(pad, x_ref, tx_ref, wx_ref, bx_ref, COLS)
    scores = lax.dot_general(c_part, b_part, (((1,), (1,)), ((), ())), preferred_element_type=jnp.float32)
    causal = lax.broadcasted_iota(jnp.int32, (rows, rows), 0) >= lax.broadcasted_iota(jnp.int32, (rows, rows), 1)
    scores = jnp.where(causal, scores, 0.0)
    low = lax.broadcasted_iota(jnp.int32, (rows, 128), 1) < HEAD_DIM
    cum = cum_ref[0]
    coef = coef_ref[0]
    zero = jnp.zeros((rows, 128), jnp.bfloat16)
    carried = []
    for j in range(0, PER_STEP, 2):
        xp = x[:, j * HEAD_DIM : (j + 2) * HEAD_DIM]
        mixes = []
        for h in (j, j + 1):
            decay = jnp.exp(jnp.minimum(cum[:, h : h + 1] - cumt_ref[0, h : h + 1, :], 0.0))
            mixes.append((scores * decay * stept_ref[0, h : h + 1, :]).astype(jnp.bfloat16))
        mix = jnp.concatenate(mixes, axis=1)
        both = jnp.concatenate([jnp.where(low, xp, zero), jnp.where(low, zero, xp)], axis=0)
        xf = xp.astype(jnp.float32)
        sl = slice(j * HEAD_DIM, (j + 2) * HEAD_DIM)
        y_ref[:, sl] = jnp.dot(mix, both, preferred_element_type=jnp.float32) + skip_ref[:, sl] * xf
        carried.append((jnp.where(low, coef[:, j : j + 1], coef[:, j + 1 : j + 2]) * xf).astype(jnp.bfloat16))
    fresh_ref[...] = lax.dot_general(
        b_part, jnp.concatenate(carried, axis=1), (((0,), (0,)), ((), ())), preferred_element_type=jnp.float32
    )


def state_kernel(live_ref, start_ref, y_ref, fresh_ref, c_ref, ecum_ref, elast_ref, y_out_ref, final_ref):
    rows = y_ref.shape[0]
    start = start_ref[...]
    start = jnp.where(live_ref[0] > 0, start, jnp.zeros_like(start))
    low = lax.broadcasted_iota(jnp.int32, (rows, 128), 1) < HEAD_DIM
    ecum = ecum_ref[0]
    ys = jnp.dot(c_ref[...], start, preferred_element_type=jnp.float32)
    for j in range(0, PER_STEP, 2):
        sl = slice(j * HEAD_DIM, (j + 2) * HEAD_DIM)
        factor = jnp.where(low, ecum[:, j : j + 1], ecum[:, j + 1 : j + 2])
        y_out_ref[:, sl] = (y_ref[:, sl] + factor * ys[:, sl]).astype(jnp.bfloat16)
    final_ref[0] = (elast_ref[...] * start.astype(jnp.float32) + fresh_ref[...]).astype(jnp.bfloat16)


def by_step(a):
    return a.reshape(a.shape[0], STEPS, PER_STEP).transpose(1, 0, 2)


def local(
    xbc, dt_raw, conv_weight, conv_bias, dt_bias, a_log, d_skip, cache_states, cache_tails,
    hit_owner, hit_slot, hit_spans, request_of,
):
    count = hit_owner.shape[0]
    rows = xbc.shape[0]
    mine = request_of[0]
    live = (hit_spans[mine] > 0).astype(jnp.int32)
    device = lax.axis_index("req")
    served = jnp.max(jnp.where(hit_owner == device, hit_slot, 0))
    own_tail = lax.dynamic_slice_in_dim(cache_tails, served, 1, 0)
    every_tail = lax.all_gather(own_tail, "req", axis=0, tiled=True)
    send = lax.dynamic_slice_in_dim(cache_states, served, 1, 0).reshape(count, NST // count, INNER)
    number = jnp.broadcast_to(mine.astype(send.dtype), send.shape[:2] + (128,))
    send, every_tail = lax.optimization_barrier((jnp.concatenate([send, number], axis=2), every_tail))
    parts = lax.all_to_all(
        send, "req", split_axis=0, concat_axis=0, tiled=True
    )
    every_request = parts[:, 0, INNER].astype(jnp.int32)
    owners = jnp.sum(
        jnp.where(every_request[:, None] == jnp.arange(count)[None, :], hit_owner[None, :], 0), axis=1
    )
    chosen = pick(parts, owners)
    start = lax.all_to_all(chosen, "req", split_axis=0, concat_axis=0, tiled=True).reshape(NST, INNER)

    tail = lax.dynamic_index_in_dim(every_tail, hit_owner[mine], 0, keepdims=False)
    tail = jnp.where(live > 0, tail, jnp.zeros_like(tail)).astype(jnp.float32)
    tail = jnp.pad(tail, ((5, 0), (0, 0)))
    step = jax.nn.softplus(dt_raw + dt_bias[None, :])
    below = jnp.tril(jnp.ones((rows, rows), jnp.float32))
    cum = jnp.dot(below, step * (-jnp.exp(a_log))[None, :], precision=lax.Precision.HIGHEST)
    last = cum[rows - 1]
    coef = jnp.exp(last[None, :] - cum) * step
    skip = jnp.repeat(d_skip, HEAD_DIM)[None, :]
    elast = jnp.repeat(jnp.exp(last), HEAD_DIM)[None, :]
    cumt = cum.T.reshape(STEPS, PER_STEP, rows)
    stept = step.T.reshape(STEPS, PER_STEP, rows)
    bias = conv_bias[None, :]

    first_b, first_c = INNER // NST, INNER // NST + GROUPS
    per = STEPS_PER_GROUP
    triple = lambda r: [
        pl.BlockSpec((r, COLS), lambda i: (0, i)),
        pl.BlockSpec((r, NST), lambda i: (0, first_b + i // per)),
        pl.BlockSpec((r, NST), lambda i: (0, first_c + i // per)),
    ]
    wide = lambda r: pl.BlockSpec((r, COLS), lambda i: (0, i))
    tall = pl.BlockSpec((1, rows, PER_STEP), lambda i: (i, 0, 0))
    flat = pl.BlockSpec((1, PER_STEP, rows), lambda i: (i, 0, 0))
    group = pl.BlockSpec((rows, NST), lambda i: (0, i // per))
    y_local, fresh, c_part = pl.pallas_call(
        local_kernel,
        grid=(STEPS,),
        out_shape=(
            jax.ShapeDtypeStruct((rows, INNER), jnp.float32),
            jax.ShapeDtypeStruct((NST, INNER), jnp.float32),
            jax.ShapeDtypeStruct((rows, GROUPS * NST), jnp.bfloat16),
        ),
        in_specs=triple(rows) + triple(8) + triple(4) + triple(1) + [tall, flat, flat, tall, wide(1)],
        out_specs=(wide(rows), wide(NST), group),
        scratch_shapes=[pltpu.VMEM((8 + rows, COLS), jnp.float32)],
        compiler_params=pltpu.CompilerParams(vmem_limit_bytes=58 * 2**20),
        cost_estimate=pl.CostEstimate(flops=10**9, bytes_accessed=40 * 10**6, transcendentals=4 * 10**6),
        name="local",
    )(xbc, xbc, xbc, tail, tail, tail, conv_weight, conv_weight, conv_weight, bias, bias, bias,
      by_step(cum), cumt, stept, by_step(coef), skip)

    return pl.pallas_call(
        state_kernel,
        grid=(STEPS,),
        out_shape=(
            jax.ShapeDtypeStruct((rows, INNER), jnp.bfloat16),
            jax.ShapeDtypeStruct((1, NST, INNER), jnp.bfloat16),
        ),
        in_specs=[pl.BlockSpec(memory_space=pltpu.SMEM), wide(NST), wide(rows), wide(NST), group, tall, wide(1)],
        out_specs=(wide(rows), pl.BlockSpec((1, NST, COLS), lambda i: (0, 0, i))),
        compiler_params=pltpu.CompilerParams(vmem_limit_bytes=14 * 2**20),
        name="state",
    )(live[None], start, y_local, fresh, c_part, by_step(jnp.exp(cum)), elast)


def solution(mesh):
    rows = P(("grp", "req"), None)
    slots = P(("grp", "req"), None, None)
    in_specs = (
        rows, rows, P(), P(), P(), P(), P(), slots, slots, P("grp"), P("grp"), P("grp"), P(("grp", "req")),
    )
    return jax.shard_map(local, mesh=mesh, in_specs=in_specs, out_specs=(rows, slots), check_vma=False)
```
